512 devices in a mesh: group: 64 (over y, z), ingroup: 8 (over x, core).
Axes of the slice: x: 4, y: 4, z: 16, core: 2. Of those that a mesh axis runs over, the one named last changes fastest.
Arguments:
- multipoles: bfloat16 [338, 65536], P(None, ('group', 'ingroup')), may hold values from -6 to 6
- interaction_lists: int32 [6, 36, 65536], P(None, None, ('group', 'ingroup')), may hold values from -1 to 671, as said below
- ghost_exports: int32 [512, 512], P(('group', 'ingroup')), may hold values from 0 to 127, as said below
- sibling_exports: int32 [512, 4], P(('group', 'ingroup')), may hold values from 0 to 127, as said below
- box_counts: int32 [512], P(('group', 'ingroup')), may hold values from 32 to 128, as said below
- multipole_to_plane: bfloat16 [1440, 338], replicated, may hold values from -0.3125 to 0.3125
- plane_shifts: float32 [6, 36, 240], replicated, may hold values from -1 to 1, as said below
- plane_to_local: bfloat16 [338, 1440], replicated, may hold values from -0.15625 to 0.15625
Outputs:
- local_expansions: bfloat16 [338, 65536], P(None, ('group', 'ingroup'))
The draws below stay inside these ranges and needn't reach their ends.
Inputs may be any that keep to these rules, and one draw needn't show every extreme that they name: `interaction_lists`: columns below 128 are live box slots of the target's own device; the others index the sibling and slab parts of its source table. `ghost_exports`: every entry is a live box slot of the exporting device, below its count. `sibling_exports`: every entry is a live box slot of the exporting device, below its count. `box_counts`: some device has exactly 128 live boxes in every draw. `plane_shifts`: each complex factor has magnitude at most 1.
All inputs are finite; a program needn't handle non-finite values.
Results may differ from the reference program's by a relative error of at most 0.0058.
Values may be sent and summed in bfloat16 or wider, within the bound.
A program may use at most 64 MiB of HBM per device.

```python
import math
import jax
import jax.numpy as jnp
from jax import lax

MREAL = 338
NODES = 120
EXP = 240
DIRS = 6
LIST = 36
SEND = 8
CAP = 128
SEND_IN = 4
TAB = 672
BOXES = 65536
N_GROUP = 64
N_INGROUP = 8
DEVICES = 512


def loads(key):
    base = jax.random.randint(jax.random.fold_in(key, 101), (DEVICES,), CAP // 4, CAP // 2 + 1)
    heavy = jax.random.randint(jax.random.fold_in(key, 102), (DEVICES,), 0, 16) == 0
    busiest = jax.random.randint(jax.random.fold_in(key, 103), (), 0, DEVICES)
    marked = heavy | (jnp.arange(DEVICES) == busiest)
    return (jnp.where(marked, CAP, base).astype(jnp.int32), busiest)


def draw_box_counts(key, part):
    counts, busiest = loads(key)
    return counts


def draw_ghost_exports(key, part):
    counts, busiest = loads(key)
    key = jax.random.fold_in(key, 2)
    drawn = jax.random.randint(key, (DEVICES, N_GROUP * SEND), 0, counts[:, None])
    drawn = drawn.at[busiest, 0].set(CAP - 1)
    drawn = drawn.at[busiest, 1].set(0)
    return drawn.astype(jnp.int32)


def draw_sibling_exports(key, part):
    counts, busiest = loads(key)
    key = jax.random.fold_in(key, 3)
    drawn = jax.random.randint(key, (DEVICES, SEND_IN), 0, counts[:, None])
    drawn = drawn.at[busiest, 0].set(CAP - 1)
    drawn = drawn.at[busiest, 1].set(0)
    return drawn.astype(jnp.int32)


def draw_interaction_lists(key, part):
    counts, busiest = loads(key)
    key = jax.random.fold_in(key, 4)
    shape = (DIRS, LIST, BOXES)
    owner_counts = jnp.repeat(counts, CAP)
    region = jax.random.randint(jax.random.fold_in(key, 11), shape, 0, 20)
    local_pick = jax.random.randint(jax.random.fold_in(key, 12), shape, 0, owner_counts[None, None, :])
    near_pick = CAP + jax.random.randint(jax.random.fold_in(key, 13), shape, 0, N_INGROUP * SEND_IN)
    far_pick = CAP + N_INGROUP * SEND_IN + jax.random.randint(jax.random.fold_in(key, 14), shape, 0, N_GROUP * SEND)
    lists = jnp.where(region < 7, -1, jnp.where(region < 12, local_pick, jnp.where(region < 15, near_pick, far_pick)))
    lists = lists.at[0, 0, 0].set(TAB - 1)
    lists = lists.at[0, 0, 1].set(-1)
    return lists.astype(jnp.int32)


def draw_plane_shifts(key, part):
    key = jax.random.fold_in(key, 6)
    shape = (DIRS, LIST, NODES)
    magnitude = jnp.exp(jax.random.uniform(jax.random.fold_in(key, 21), shape, jnp.float32, math.log(0.05), 0.0))
    phase = jax.random.uniform(jax.random.fold_in(key, 22), shape, jnp.float32, -math.pi, math.pi)
    return jnp.concatenate([magnitude * jnp.cos(phase), magnitude * jnp.sin(phase)], axis=-1).astype(jnp.float32)


def levels(key, extent, split, low, largest):
    def one(axis_at, parts):
        heights = jax.random.uniform(jax.random.fold_in(jax.random.fold_in(key, 6), axis_at), (parts,), jnp.float32, low / len(split), largest / len(split))
        return jnp.repeat(jnp.exp(heights), extent[axis_at] // parts).reshape((-1,) + (1,) * (len(extent) - axis_at - 1))

    gain = one(*split[0])
    for cut in split[1:]:
        gain = gain * one(*cut)
    return gain


def noise(key, extent, scale, most, shards=(), held_as=jnp.bfloat16):
    entries = jax.random.normal(key, extent, jnp.float32) * scale
    if len(shards) > 0:
        entries = levels(key, extent, shards, -0.22, 0.18) * entries
    return jnp.clip(entries, min=-most, max=most).astype(held_as)


def setup_inputs(seed: int = 0) -> dict:
    streams_of = jax.random.split(jax.random.key(seed), 9)
    multipoles = noise(streams_of[0], (MREAL, BOXES), 1.0, 6.0, ((1, 512),))
    interaction_lists = draw_interaction_lists(jax.random.fold_in(streams_of[8], 71), 0)
    ghost_exports = draw_ghost_exports(jax.random.fold_in(streams_of[8], 71), 0)
    sibling_exports = draw_sibling_exports(jax.random.fold_in(streams_of[8], 71), 0)
    box_counts = draw_box_counts(jax.random.fold_in(streams_of[8], 71), 0)
    multipole_to_plane = noise(streams_of[5], (DIRS * EXP, MREAL), MREAL ** -0.5, 0.3125)
    plane_shifts = draw_plane_shifts(jax.random.fold_in(streams_of[8], 71), 0)
    plane_to_local = noise(streams_of[7], (MREAL, DIRS * EXP), (DIRS * EXP) ** -0.5, 0.15625)
    return {"multipoles": multipoles, "interaction_lists": interaction_lists, "ghost_exports": ghost_exports, "sibling_exports": sibling_exports, "box_counts": box_counts, "multipole_to_plane": multipole_to_plane, "plane_shifts": plane_shifts, "plane_to_local": plane_to_local}


def exponential(box_table, slot_lists, plane_shifts):
    pieces = []
    for direction in range(DIRS):
        plane_rows = box_table[direction * EXP:(direction + 1) * EXP]
        safe_slots = jnp.maximum(slot_lists[direction], 0)
        picked = jnp.take(plane_rows, safe_slots, axis=1).astype(jnp.float32)
        picked = jnp.where((slot_lists[direction] >= 0)[None], picked, jnp.float32(0.0))
        real_factor = plane_shifts[direction, :, :NODES].T[:, :, None]
        imaginary_factor = plane_shifts[direction, :, NODES:].T[:, :, None]
        real_part = picked[:NODES]
        imaginary_part = picked[NODES:]
        real_sum = jnp.sum(real_factor * real_part - imaginary_factor * imaginary_part, axis=1)
        imaginary_sum = jnp.sum(real_factor * imaginary_part + imaginary_factor * real_part, axis=1)
        pieces.append(real_sum)
        pieces.append(imaginary_sum)
    return jnp.concatenate(pieces, axis=0).astype(jnp.bfloat16)


def reference(multipoles, interaction_lists, ghost_exports, sibling_exports, box_counts, multipole_to_plane, plane_shifts, plane_to_local):
    by_device = jnp.moveaxis(multipoles.reshape(MREAL, DEVICES, CAP), 1, 0)

    def convert(columns):
        return jnp.dot(multipole_to_plane, columns, preferred_element_type=jnp.float32).astype(jnp.bfloat16)

    planes = lax.map(convert, by_device)
    slab_exports = ghost_exports.reshape(DEVICES, N_GROUP, SEND)

    def one_device(device):
        slab_index = device // N_INGROUP
        member = device % N_INGROUP
        own_planes = planes[device]
        siblings = slab_index * N_INGROUP + jnp.arange(N_INGROUP, dtype=jnp.int32)
        near_slots = sibling_exports[siblings]
        sibling = planes[siblings[:, None], :, near_slots].reshape(-1, DIRS * EXP).T
        sources = jnp.arange(N_GROUP, dtype=jnp.int32) * N_INGROUP + member
        far_slots = slab_exports[sources, slab_index]
        remote = planes[sources[:, None], :, far_slots].reshape(-1, DIRS * EXP).T
        source_table = jnp.concatenate([own_planes, sibling, remote], axis=1)
        slot_lists = lax.dynamic_slice_in_dim(interaction_lists, device * CAP, CAP, 2)
        exponentials = exponential(source_table, slot_lists, plane_shifts)
        local_terms = jnp.dot(plane_to_local, exponentials, preferred_element_type=jnp.float32)
        live_mask = jnp.arange(CAP, dtype=jnp.int32) < box_counts[device]
        return jnp.where(live_mask[None], local_terms, jnp.float32(0.0)).astype(jnp.bfloat16)

    result = lax.map(one_device, jnp.arange(DEVICES, dtype=jnp.int32))
    return jnp.moveaxis(result, 0, 1).reshape(MREAL, BOXES)
```

```python
import functools

import jax
import jax.numpy as jnp
from jax import lax
from jax.experimental import pallas as pl
from jax.experimental.pallas import tpu as pltpu
from jax.sharding import PartitionSpec as P

MESH = pl.DeviceIdType.MESH
BF16, F32, I32 = jnp.bfloat16, jnp.float32, jnp.int32

LANES = 128
TILE = 256
NY, NZ = 4, 16
NSIB = 8
STACK = 4
WIDE = 384
SERVE = ((6, 7), (0, 3), (3, 3))


def columns_of(row, count):
    wide = jnp.broadcast_to(row.astype(F32), (LANES, count))
    return jnp.concatenate([wide[:, c : c + LANES].T for c in range(0, count, LANES)], axis=0)


def kernel(
    mult_ref, lists_ref, ghost_ref, sibx_ref, count_ref, m2p_ref, shifts_ref, p2l_ref, out_ref,
    mult_pad, m2p_pad, p2l_pad, shift_pad, rel, send, sib_send, own_x, sib_recv, recv, planes, acc,
    send_sem, sib_send_sem, sib_sem, tile_sem, in1_sem, in2_sem, go1_sem, go2_sem,
):
    g = lax.axis_index("group")
    i = lax.axis_index("ingroup")
    y, z = g // NZ, lax.rem(g, NZ)
    first, second, third = z < 4, (z >= 4) & (z < 8), z >= 8
    low = z < 8
    dirs, slots = lists_ref.shape[0], lists_ref.shape[1]
    mreal, cap = mult_ref.shape
    nodes = shifts_ref.shape[2] // 2

    def signal(sem, slab):
        pl.semaphore_signal(sem, 1, device_id=(slab, i), device_id_type=MESH)

    barrier = pltpu.get_barrier_semaphore()

    def greet_sibling(n, c):
        pl.semaphore_signal(barrier, 1, device_id=(g, lax.rem(i + n, NSIB)), device_id_type=MESH)
        return c

    lax.fori_loop(1, NSIB, greet_sibling, 0)

    @pl.when(first)
    def _():
        def greet(n, c):
            signal(barrier, lax.rem(g + n, NY * NZ))
            return c

        lax.fori_loop(1, NY * NZ, greet, 0)

    mult_pad[...] = jnp.zeros_like(mult_pad)
    mult_pad[:mreal, :] = mult_ref[...]
    lane = lax.broadcasted_iota(I32, (LANES, LANES), 1).astype(F32)

    def pick(cols):
        lanes = lax.broadcasted_iota(I32, cols.shape, 1).astype(F32)
        hot = jnp.where(cols == lanes, F32(1), F32(0)).astype(BF16)
        rows = lax.dot_general(hot, mult_pad[...], (((1,), (1,)), ((), ())), preferred_element_type=F32)
        return rows.astype(BF16)

    n_ghost = ghost_ref.shape[1]
    send[...] = pick(columns_of(ghost_ref[...], n_ghost)).reshape(send.shape)
    sib_row = jnp.concatenate([sibx_ref[...], jnp.full((1, LANES - sibx_ref.shape[1]), -1, I32)], axis=1)
    sib_send[...] = pick(columns_of(sib_row, LANES)[: sib_send.shape[0]])
    sib_recv[i] = sib_send[...]

    @pl.when(low)
    def _():
        recv[0, y * 8 + lax.rem(z, 8)] = send[g]

    @pl.when(third)
    def _():
        recv[1, y * 8 + lax.rem(z, 8)] = send[g]

    @pl.when(first)
    def _():
        pl.semaphore_wait(barrier, 7 + 15)

    @pl.when(jnp.logical_not(first))
    def _():
        pl.semaphore_wait(barrier, 7 + 16)

    def report(sem):
        def one(n, c):
            signal(sem, lax.rem(y + n // 4, NY) * NZ + lax.rem(n, 4))
            return c

        lax.fori_loop(0, 16, one, 0)

    @pl.when(second)
    def _():
        report(in1_sem)

    @pl.when(third)
    def _():
        report(in2_sem)

    side = z // 8
    slot = y * 8 + lax.rem(z, 8)

    def send_to(slab):
        @pl.when(slab != g)
        def _():
            pltpu.make_async_remote_copy(
                src_ref=send.at[slab],
                dst_ref=recv.at[side, slot],
                send_sem=send_sem,
                recv_sem=tile_sem.at[side],
                device_id=(slab, i),
                device_id_type=MESH,
            ).start()

    def send_sib(n, c):
        pltpu.make_async_remote_copy(
            src_ref=sib_send,
            dst_ref=sib_recv.at[i],
            send_sem=sib_send_sem,
            recv_sem=sib_sem,
            device_id=(g, lax.rem(i + n, NSIB)),
            device_id_type=MESH,
        ).start()
        return c

    lax.fori_loop(1, NSIB, send_sib, 0)

    def serve(base, width):
        def one(n, c):
            zz = n // NY
            if width == 8:
                zz = lax.rem(zz + z, 8)
            send_to(lax.rem(y + n, NY) * NZ + base + zz)
            return c

        lax.fori_loop(0, NY * width, one, 0)

    serve(0, 4)

    own_x[...] = jnp.zeros_like(own_x)
    own_x[:cap] = pick(lax.broadcasted_iota(I32, (LANES, LANES), 0).astype(F32))
    m2p_pad[...] = jnp.zeros_like(m2p_pad)
    p2l_pad[...] = jnp.zeros_like(p2l_pad)
    shift_pad[...] = jnp.zeros_like(shift_pad)
    acc[...] = jnp.zeros_like(acc)
    for d in range(dirs):
        for h in range(2):
            at = (2 * d + h) * nodes
            m2p_pad[d, h * LANES : h * LANES + nodes, :mreal] = m2p_ref[at : at + nodes, :]
            p2l_pad[d, :, h * LANES : h * LANES + nodes] = p2l_ref[:, at : at + nodes]
            shift_pad[d, :slots, h * LANES : h * LANES + nodes] = shifts_ref[d, :, h * nodes : (h + 1) * nodes]
        lists = lists_ref[d]
        far = lists - (cap + NSIB * 4)
        near = lists - cap
        far_at = lax.shift_right_arithmetic(far, 7) * 64 + (far & 63)
        upper = (far & 64) != 0
        own_at = jnp.where(lists < cap, lists, cap + lax.shift_right_arithmetic(near, 2) * 8 + (near & 3))
        none = jnp.full_like(lists, -1)
        for tile, place in enumerate((
            jnp.where(far < 0, jnp.where(lists < 0, none, own_at), none),
            jnp.where((far >= 0) & jnp.logical_not(upper), far_at, none),
            jnp.where((far >= 0) & upper, far_at, none),
        )):
            place = jnp.concatenate([place, jnp.full((40 - slots, cap), -1, I32)], axis=0)
            rel[tile, d, :, :40] = place.astype(F32).T.astype(BF16)

    def wait_all(ref, sem):
        pltpu.make_async_copy(ref, ref, sem).wait()

    def convert(rows):
        def one(d, c):
            made = lax.dot_general(rows, m2p_pad[d], (((1,), (1,)), ((), ())), preferred_element_type=F32)
            planes[d] = made.astype(BF16)
            return c

        lax.fori_loop(0, dirs, one, 0)

    def step(q, c):
        tile, d = q // dirs, lax.rem(q, dirs)

        def at(cond, when, action):
            @pl.when(cond & (q == when))
            def _():
                action()

        def first_to_second():
            pl.semaphore_wait(in1_sem, 16)
            signal(go1_sem, g + 4)
            serve(4, 4)

        def first_to_third():
            pl.semaphore_wait(in2_sem, 32)
            for ahead in (4, 8, 12):
                signal(go2_sem, g + ahead)
            serve(8, 8)

        def second_to_second():
            pl.semaphore_wait(go1_sem, 1)
            serve(4, 4)

        def second_to_third():
            pl.semaphore_wait(go2_sem, 1)
            serve(8, 8)

        def third_to_rest():
            pl.semaphore_wait(go2_sem, 1)
            serve(4, 4)
            serve(8, 8)

        at(first, SERVE[0][0], first_to_second)
        at(first, SERVE[0][1], first_to_third)
        at(second, SERVE[1][0], second_to_second)
        at(second, SERVE[1][1], second_to_third)
        at(third, SERVE[2][0], third_to_rest)

        @pl.when(q == 0)
        def _():
            wait_all(sib_recv.at[pl.ds(0, 7)], sib_sem)
            own_x[cap : cap + 64] = sib_recv[...].reshape(64, WIDE)
            convert(own_x[...])

        def far_tile(when, which, mine):
            @pl.when((q == when) & mine)
            def _():
                wait_all(recv.at[which, pl.ds(0, 31)], tile_sem.at[which])

            @pl.when((q == when) & jnp.logical_not(mine))
            def _():
                wait_all(recv.at[which], tile_sem.at[which])

            @pl.when(q == when)
            def _():
                convert(recv[which].reshape(TILE, WIDE))

        far_tile(dirs, 0, low)
        far_tile(2 * dirs, 1, third)

        sources = lax.broadcasted_iota(I32, (cap, TILE), 1).astype(F32).astype(BF16)
        table = planes[d]
        real = acc[d, :, :LANES]
        imaginary = acc[d, :, LANES:]
        for j0 in range(0, slots, STACK):
            hot = jnp.concatenate(
                [jnp.where(sources == rel[tile, d, :, j : j + 1], BF16(1), BF16(0)) for j in range(j0, j0 + STACK)],
                axis=0,
            )
            picked = jnp.dot(hot, table, preferred_element_type=F32)
            for n in range(STACK):
                j = j0 + n
                sr, si = shift_pad[d, j : j + 1, :LANES], shift_pad[d, j : j + 1, LANES:]
                pr, pi = picked[n * cap : (n + 1) * cap, :LANES], picked[n * cap : (n + 1) * cap, LANES:]
                real = real + sr * pr - si * pi
                imaginary = imaginary + sr * pi + si * pr
        acc[d, :, :LANES] = real
        acc[d, :, LANES:] = imaginary
        return c

    lax.fori_loop(0, 3 * dirs, step, 0)

    total = jnp.zeros((mreal, cap), F32)
    for d in range(dirs):
        total = total + lax.dot_general(
            p2l_pad[d], acc[d].astype(BF16), (((1,), (1,)), ((), ())), preferred_element_type=F32
        )
    live = lax.broadcasted_iota(I32, (mreal, cap), 1) < count_ref[0]
    out_ref[...] = jnp.where(live, total, F32(0)).astype(BF16)

    wait_all(send.at[pl.ds(0, NY * NZ - 1)], send_sem)
    wait_all(sib_recv.at[pl.ds(0, 7)], sib_send_sem)


def per_device(mult, lists, ghost, sibx, counts, m2p, shifts, p2l):
    mreal, cap = mult.shape
    dirs = lists.shape[0]
    vmem = pl.BlockSpec(memory_space=pltpu.VMEM)
    return pl.pallas_call(
        kernel,
        out_shape=jax.ShapeDtypeStruct((mreal, cap), BF16),
        in_specs=[vmem] * 4 + [pl.BlockSpec(memory_space=pltpu.SMEM)] + [vmem] * 3,
        out_specs=vmem,
        scratch_shapes=[
            pltpu.VMEM((WIDE, cap), BF16),
            pltpu.VMEM((dirs, TILE, WIDE), BF16),
            pltpu.VMEM((dirs, mreal, TILE), BF16),
            pltpu.VMEM((dirs, 40, TILE), F32),
            pltpu.VMEM((3, dirs, cap, LANES), BF16),
            pltpu.VMEM((NY * NZ, 8, WIDE), BF16),
            pltpu.VMEM((8, WIDE), BF16),
            pltpu.VMEM((TILE, WIDE), BF16),
            pltpu.VMEM((NSIB, 8, WIDE), BF16),
            pltpu.VMEM((2, 32, 8, WIDE), BF16),
            pltpu.VMEM((dirs, TILE, TILE), BF16),
            pltpu.VMEM((dirs, cap, TILE), F32),
            pltpu.SemaphoreType.DMA,
            pltpu.SemaphoreType.DMA,
            pltpu.SemaphoreType.DMA,
            pltpu.SemaphoreType.DMA((2,)),
            pltpu.SemaphoreType.REGULAR,
            pltpu.SemaphoreType.REGULAR,
            pltpu.SemaphoreType.REGULAR,
            pltpu.SemaphoreType.REGULAR,
        ],
        compiler_params=pltpu.CompilerParams(
            collective_id=0, has_side_effects=True, vmem_limit_bytes=40 * 2**20
        ),
        cost_estimate=pl.CostEstimate(flops=12 * 10**9, bytes_accessed=3 * 10**6, transcendentals=0),
    )(mult, lists, ghost, sibx, counts, m2p, shifts, p2l)


def solution(mesh):
    both = ("group", "ingroup")
    return jax.shard_map(
        per_device,
        mesh=mesh,
        in_specs=(P(None, both), P(None, None, both), P(both, None), P(both, None), P(both), P(), P(), P()),
        out_specs=P(None, both),
        check_vma=False,
    )
```

```python
import functools

import jax
import jax.numpy as jnp
from jax import lax
from jax.experimental import pallas as pl
from jax.experimental.pallas import tpu as pltpu
from jax.sharding import PartitionSpec as P

MESH = pl.DeviceIdType.MESH
BF16, F32, I32 = jnp.bfloat16, jnp.float32, jnp.int32

LANES = 128
TILE = 256
NY, NZ = 4, 16
NSIB = 8
STACK = 2
WIDE = 384
HALF = 8


def columns_of(row, count):
    wide = jnp.broadcast_to(row.astype(F32), (LANES, count))
    return jnp.concatenate([wide[:, c : c + LANES].T for c in range(0, count, LANES)], axis=0)


def kernel(
    mult_hbm, ghost_hbm, sibx_hbm, count_hbm, lists_hbm, m2p_hbm, shifts_hbm, p2l_hbm, out_ref,
    mult_ref, ghost_ref, sibx_ref, count_ref, lists_ref, m2p_ref, shifts_ref, p2l_ref,
    mult_pad, m2p_pad, p2l_pad, shift_pad, place_cols, places, send, sib_send, rows, sib_recv, recv, planes, acc,
    send_sem, sib_send_sem, sib_sem, tile_sem, load_sem,
):
    g = lax.axis_index("group")
    i = lax.axis_index("ingroup")
    y, z = g // NZ, lax.rem(g, NZ)
    low = z < HALF
    side = z // HALF
    slot = y * HALF + lax.rem(z, HALF)
    dirs, slots = lists_ref.shape[0], lists_ref.shape[1]
    mreal, cap = mult_ref.shape
    nodes = shifts_ref.shape[2] // 2

    barrier = pltpu.get_barrier_semaphore()

    loads = [
        pltpu.make_async_copy(src, dst, load_sem.at[n])
        for n, (src, dst) in enumerate((
            (ghost_hbm, ghost_ref), (mult_hbm, mult_ref), (sibx_hbm, sibx_ref), (count_hbm, count_ref),
            (lists_hbm, lists_ref), (m2p_hbm, m2p_ref), (shifts_hbm, shifts_ref), (p2l_hbm, p2l_ref),
        ))
    ]
    for load in loads:
        load.start()

    def greet_slab(n, c):
        slab = ((y + n) & (NY - 1)) * NZ + ((z + n // NY) & (NZ - 1))
        pl.semaphore_signal(barrier, 1, device_id=(slab, i), device_id_type=MESH)
        return c

    def greet_sibling(n, c):
        pl.semaphore_signal(barrier, 1, device_id=(g, (i + n) & (NSIB - 1)), device_id_type=MESH)
        return c

    lax.fori_loop(1, NY * NZ, greet_slab, 0)
    lax.fori_loop(1, NSIB, greet_sibling, 0)

    mult_pad[...] = jnp.zeros_like(mult_pad)
    for load in loads[:4]:
        load.wait()
    mult_pad[:mreal, :] = mult_ref[...]

    def pick(cols):
        lanes = lax.broadcasted_iota(I32, cols.shape, 1).astype(F32)
        hot = jnp.where(cols == lanes, F32(1), F32(0)).astype(BF16)
        made = lax.dot_general(hot, mult_pad[...], (((1,), (1,)), ((), ())), preferred_element_type=F32)
        return made.astype(BF16)

    n_ghost = ghost_ref.shape[1]
    send[...] = pick(columns_of(ghost_ref[...], n_ghost)).reshape(send.shape)
    sib_row = jnp.concatenate([sibx_ref[...], jnp.full((1, LANES - sibx_ref.shape[1]), -1, I32)], axis=1)
    sib_send[...] = pick(columns_of(sib_row, LANES)[: sib_send.shape[0]])
    sib_recv[i] = sib_send[...]
    recv[side, slot] = send[g]

    lower = lax.broadcasted_iota(I32, (cap, LANES), 1).astype(F32)
    upper = (lower + LANES).astype(BF16)
    lower = lower.astype(BF16)

    def hot_rows(tile, d, j):
        place = places[tile, d, j]
        halves = [jnp.where(lanes == place, BF16(1), BF16(0)) for lanes in (lower, upper)]
        return jnp.concatenate(halves, axis=1)

    def prepare():
        rows[...] = jnp.zeros_like(rows)
        rows[:cap] = pick(lax.broadcasted_iota(I32, (LANES, LANES), 0).astype(F32))
        m2p_pad[...] = jnp.zeros_like(m2p_pad)
        p2l_pad[...] = jnp.zeros_like(p2l_pad)
        shift_pad[...] = jnp.zeros_like(shift_pad)
        acc[...] = jnp.zeros_like(acc)
        for load in loads[4:]:
            load.wait()
        for d in range(dirs):
            for h in range(2):
                at = (2 * d + h) * nodes
                m2p_pad[d, :mreal, h * LANES : h * LANES + nodes] = m2p_ref[:, at : at + nodes]
                p2l_pad[d, :, h * LANES : h * LANES + nodes] = p2l_ref[:, at : at + nodes]
                shift_pad[d, :slots, h * LANES : h * LANES + nodes] = shifts_ref[d, :, h * nodes : (h + 1) * nodes]
            lists = lists_ref[d]
            far = lists - (cap + NSIB * 4)
            near = lists - cap
            far_at = lax.shift_right_arithmetic(far, 7) * 64 + (far & 63)
            far_side = lax.shift_right_arithmetic(far, 6) & 1
            own_at = jnp.where(lists < cap, lists, cap + lax.shift_right_arithmetic(near, 2) * 8 + (near & 3))
            far_at = far_at + jnp.where(far_side == side, TILE, 2 * TILE)
            place = jnp.where(far < 0, own_at, far_at)
            place = jnp.concatenate([place, jnp.full((40 - slots, cap), -1, I32)], axis=0)
            place_cols[d] = place.astype(F32).T

        def spread(d, c):
            for j in range(slots):
                place = jnp.broadcast_to(place_cols[d, :, j : j + 1], (cap, LANES))
                for tile in range(3):
                    places[tile, d, j] = (place - F32(tile * TILE)).astype(BF16)
            return c

        lax.fori_loop(0, dirs, spread, 0)

    def send_all():
        pl.semaphore_wait(barrier, NY * NZ - 1 + NSIB - 1)

        def send_sib(n, c):
            pltpu.make_async_remote_copy(
                src_ref=sib_send,
                dst_ref=sib_recv.at[i],
                send_sem=sib_send_sem,
                recv_sem=sib_sem,
                device_id=(g, (i + n) & (NSIB - 1)),
                device_id_type=MESH,
            ).start()
            return c

        lax.fori_loop(1, NSIB, send_sib, 0)

        def send_slab(n, c):
            to_z = (n // (NY * HALF)) * HALF + ((n // NY + z) & (HALF - 1))
            slab = ((y + n) & (NY - 1)) * NZ + to_z

            @pl.when(slab != g)
            def _():
                pltpu.make_async_remote_copy(
                    src_ref=send.at[slab],
                    dst_ref=recv.at[side, slot],
                    send_sem=send_sem,
                    recv_sem=tile_sem.at[jnp.where(to_z // HALF == side, 0, 1)],
                    device_id=(slab, i),
                    device_id_type=MESH,
                ).start()

            return c

        lax.fori_loop(0, NY * NZ, send_slab, 0)

    def turn(n, c):
        @pl.when((n == 0) == low)
        def _():
            prepare()

        @pl.when((n == 0) != low)
        def _():
            send_all()

        return c

    lax.fori_loop(0, 2, turn, 0)

    def wait_all(ref, sem):
        pltpu.make_async_copy(ref, ref, sem).wait()

    def convert():
        for d in range(dirs):
            planes[d] = jnp.dot(rows[...], m2p_pad[d], preferred_element_type=F32).astype(BF16)

    def add_shifted(tile, d):
        table = planes[d]
        real = acc[d, :, :LANES]
        imaginary = acc[d, :, LANES:]
        for j0 in range(0, slots, STACK):
            hot = jnp.concatenate([hot_rows(tile, d, j) for j in range(j0, j0 + STACK)], axis=0)
            picked = jnp.dot(hot, table, preferred_element_type=F32)
            for n in range(STACK):
                j = j0 + n
                sr, si = shift_pad[d, j : j + 1, :LANES], shift_pad[d, j : j + 1, LANES:]
                pr, pi = picked[n * cap : (n + 1) * cap, :LANES], picked[n * cap : (n + 1) * cap, LANES:]
                real = real + sr * pr - si * pi
                imaginary = imaginary + sr * pi + si * pr
        acc[d, :, :LANES] = real
        acc[d, :, LANES:] = imaginary

    def step(q, c):
        tile, d = q // dirs, lax.rem(q, dirs)

        @pl.when(q == 0)
        def _():
            wait_all(sib_recv.at[pl.ds(0, NSIB - 1)], sib_sem)
            rows[cap : cap + 64] = sib_recv[...].reshape(64, WIDE)

        @pl.when(q == dirs)
        def _():
            wait_all(recv.at[0, pl.ds(0, 31)], tile_sem.at[0])
            rows[...] = recv[side].reshape(TILE, WIDE)

        @pl.when(q == 2 * dirs)
        def _():
            wait_all(recv.at[0], tile_sem.at[1])
            rows[...] = recv[1 - side].reshape(TILE, WIDE)

        @pl.when(d == 0)
        def _():
            convert()

        add_shifted(tile, d)
        return c

    lax.fori_loop(0, 3 * dirs, step, 0)

    total = jnp.zeros((mreal, cap), F32)
    for d in range(dirs):
        total = total + lax.dot_general(
            p2l_pad[d], acc[d].astype(BF16), (((1,), (1,)), ((), ())), preferred_element_type=F32
        )
    live = lax.broadcasted_iota(I32, (mreal, cap), 1) < count_ref[...]
    out_ref[...] = jnp.where(live, total, F32(0)).astype(BF16)

    wait_all(send.at[pl.ds(0, NY * NZ - 1)], send_sem)
    wait_all(sib_recv.at[pl.ds(0, NSIB - 1)], sib_send_sem)


def per_device(mult, lists, ghost, sibx, counts, m2p, shifts, p2l):
    mreal, cap = mult.shape
    dirs = lists.shape[0]
    width = m2p.shape[0]
    hbm = pl.BlockSpec(memory_space=pltpu.HBM)
    return pl.pallas_call(
        kernel,
        out_shape=jax.ShapeDtypeStruct((mreal, cap), BF16),
        in_specs=[hbm] * 8,
        out_specs=pl.BlockSpec(memory_space=pltpu.VMEM),
        scratch_shapes=[
            pltpu.VMEM((mreal, cap), BF16),
            pltpu.VMEM(ghost.shape, I32),
            pltpu.VMEM(sibx.shape, I32),
            pltpu.VMEM((1, 1), I32),
            pltpu.VMEM(lists.shape, I32),
            pltpu.VMEM((mreal, width), BF16),
            pltpu.VMEM(shifts.shape, F32),
            pltpu.VMEM((mreal, width), BF16),
            pltpu.VMEM((WIDE, cap), BF16),
            pltpu.VMEM((dirs, WIDE, TILE), BF16),
            pltpu.VMEM((dirs, mreal, TILE), BF16),
            pltpu.VMEM((dirs, 40, TILE), F32),
            pltpu.VMEM((dirs, cap, 40), F32),
            pltpu.VMEM((3, dirs, lists.shape[1], cap, LANES), BF16),
            pltpu.VMEM((NY * NZ, 8, WIDE), BF16),
            pltpu.VMEM((8, WIDE), BF16),
            pltpu.VMEM((TILE, WIDE), BF16),
            pltpu.VMEM((NSIB, 8, WIDE), BF16),
            pltpu.VMEM((2, NY * HALF, 8, WIDE), BF16),
            pltpu.VMEM((dirs, TILE, TILE), BF16),
            pltpu.VMEM((dirs, cap, TILE), F32),
            pltpu.SemaphoreType.DMA,
            pltpu.SemaphoreType.DMA,
            pltpu.SemaphoreType.DMA,
            pltpu.SemaphoreType.DMA((2,)),
            pltpu.SemaphoreType.DMA((8,)),
        ],
        compiler_params=pltpu.CompilerParams(
            collective_id=0, has_side_effects=True, vmem_limit_bytes=48 * 2**20
        ),
        cost_estimate=pl.CostEstimate(flops=12 * 10**9, bytes_accessed=3 * 10**6, transcendentals=0),
    )(mult, ghost, sibx, counts.reshape(1, 1), lists, m2p.T, shifts, p2l)


def solution(mesh):
    both = ("group", "ingroup")
    return jax.shard_map(
        per_device,
        mesh=mesh,
        in_specs=(P(None, both), P(None, None, both), P(both, None), P(both, None), P(both), P(), P(), P()),
        out_specs=P(None, both),
        check_vma=False,
    )
```

```python
import functools

import jax
import jax.numpy as jnp
from jax import lax
from jax.experimental import pallas as pl
from jax.experimental.pallas import tpu as pltpu
from jax.sharding import PartitionSpec as P

MESH = pl.DeviceIdType.MESH
BF16, F32, I32 = jnp.bfloat16, jnp.float32, jnp.int32

LANES = 128
TILE = 256
NY, NZ = 4, 16
NSIB = 8
STACK = 2
WIDE = 384
HALF = 8


def columns_of(row, count):
    wide = jnp.broadcast_to(row.astype(F32), (LANES, count))
    return jnp.concatenate([wide[:, c : c + LANES].T for c in range(0, count, LANES)], axis=0)


def kernel(
    mult_hbm, ghost_hbm, sibx_hbm, count_hbm, lists_hbm, m2p_hbm, shifts_hbm, p2l_hbm, out_ref,
    mult_ref, ghost_ref, sibx_ref, count_ref, lists_ref, m2p_ref, shifts_ref, p2l_ref,
    mult_pad, m2p_pad, p2l_pad, shift_pad, place_cols, places, send, sib_send, rows, sib_recv, recv, planes, acc,
    send_sem, sib_send_sem, sib_sem, tile_sem, load_sem,
):
    g = lax.axis_index("group")
    i = lax.axis_index("ingroup")
    y, z = g // NZ, lax.rem(g, NZ)
    low = z < HALF
    side = z // HALF
    slot = y * HALF + lax.rem(z, HALF)
    dirs, slots = lists_ref.shape[0], lists_ref.shape[1]
    mreal, cap = mult_ref.shape
    nodes = shifts_ref.shape[2] // 2

    barrier = pltpu.get_barrier_semaphore()

    loads = [
        pltpu.make_async_copy(src, dst, load_sem.at[n])
        for n, (src, dst) in enumerate((
            (ghost_hbm, ghost_ref), (mult_hbm, mult_ref), (sibx_hbm, sibx_ref), (count_hbm, count_ref),
            (lists_hbm, lists_ref), (m2p_hbm, m2p_ref), (shifts_hbm, shifts_ref), (p2l_hbm, p2l_ref),
        ))
    ]
    for load in loads:
        load.start()

    def greet_slab(n, c):
        slab = ((y + n) & (NY - 1)) * NZ + ((z + n // NY) & (NZ - 1))
        pl.semaphore_signal(barrier, 1, device_id=(slab, i), device_id_type=MESH)
        return c

    def greet_sibling(n, c):
        pl.semaphore_signal(barrier, 1, device_id=(g, (i + n) & (NSIB - 1)), device_id_type=MESH)
        return c

    lax.fori_loop(1, NY * NZ, greet_slab, 0)
    lax.fori_loop(1, NSIB, greet_sibling, 0)

    mult_pad[...] = jnp.zeros_like(mult_pad)
    for load in loads[:4]:
        load.wait()
    mult_pad[:mreal, :] = mult_ref[...]

    def pick(cols):
        lanes = lax.broadcasted_iota(I32, cols.shape, 1).astype(F32)
        hot = jnp.where(cols == lanes, F32(1), F32(0)).astype(BF16)
        made = lax.dot_general(hot, mult_pad[...], (((1,), (1,)), ((), ())), preferred_element_type=F32)
        return made.astype(BF16)

    n_ghost = ghost_ref.shape[1]
    send[...] = pick(columns_of(ghost_ref[...], n_ghost)).reshape(send.shape)
    sib_row = jnp.concatenate([sibx_ref[...], jnp.full((1, LANES - sibx_ref.shape[1]), -1, I32)], axis=1)
    sib_send[...] = pick(columns_of(sib_row, LANES)[: sib_send.shape[0]])
    sib_recv[i] = sib_send[...]
    recv[side, slot] = send[g]

    lower = lax.broadcasted_iota(I32, (cap, LANES), 1).astype(F32)
    upper = (lower + LANES).astype(BF16)
    lower = lower.astype(BF16)

    def hot_rows(tiles, d, j):
        halves = [
            jnp.where(lanes == places[tile, d, j], BF16(1), BF16(0)) for tile in tiles for lanes in (lower, upper)
        ]
        return jnp.concatenate(halves, axis=1)

    def prepare():
        rows[...] = jnp.zeros_like(rows)
        rows[:cap] = pick(lax.broadcasted_iota(I32, (LANES, LANES), 0).astype(F32))
        m2p_pad[...] = jnp.zeros_like(m2p_pad)
        p2l_pad[...] = jnp.zeros_like(p2l_pad)
        shift_pad[...] = jnp.zeros_like(shift_pad)
        acc[...] = jnp.zeros_like(acc)
        for load in loads[4:]:
            load.wait()
        for d in range(dirs):
            for h in range(2):
                at = (2 * d + h) * nodes
                m2p_pad[d, :mreal, h * LANES : h * LANES + nodes] = m2p_ref[:, at : at + nodes]
                p2l_pad[d, :, h * LANES : h * LANES + nodes] = p2l_ref[:, at : at + nodes]
                shift_pad[d, :slots, h * LANES : h * LANES + nodes] = shifts_ref[d, :, h * nodes : (h + 1) * nodes]
            lists = lists_ref[d]
            far = lists - (cap + NSIB * 4)
            near = lists - cap
            far_at = lax.shift_right_arithmetic(far, 7) * 64 + (far & 63)
            far_side = lax.shift_right_arithmetic(far, 6) & 1
            own_at = jnp.where(lists < cap, lists, cap + lax.shift_right_arithmetic(near, 2) * 8 + (near & 3))
            far_at = far_at + jnp.where(far_side == side, TILE, 2 * TILE)
            place = jnp.where(far < 0, own_at, far_at)
            place = jnp.concatenate([place, jnp.full((40 - slots, cap), -1, I32)], axis=0)
            place_cols[d] = place.astype(F32).T

        def spread(d, c):
            for j in range(slots):
                place = jnp.broadcast_to(place_cols[d, :, j : j + 1], (cap, LANES))
                for tile in range(3):
                    places[tile, d, j] = (place - F32(tile * TILE)).astype(BF16)
            return c

        lax.fori_loop(0, dirs, spread, 0)

    def send_all():
        pl.semaphore_wait(barrier, NY * NZ - 1 + NSIB - 1)

        def send_sib(n, c):
            pltpu.make_async_remote_copy(
                src_ref=sib_send,
                dst_ref=sib_recv.at[i],
                send_sem=sib_send_sem,
                recv_sem=sib_sem,
                device_id=(g, (i + n) & (NSIB - 1)),
                device_id_type=MESH,
            ).start()
            return c

        lax.fori_loop(1, NSIB, send_sib, 0)

        def send_slab(n, c):
            to_z = (n // (NY * HALF)) * HALF + ((n // NY + z) & (HALF - 1))
            slab = ((y + n) & (NY - 1)) * NZ + to_z

            @pl.when(slab != g)
            def _():
                pltpu.make_async_remote_copy(
                    src_ref=send.at[slab],
                    dst_ref=recv.at[side, slot],
                    send_sem=send_sem,
                    recv_sem=tile_sem.at[jnp.where(to_z // HALF == side, 0, 1)],
                    device_id=(slab, i),
                    device_id_type=MESH,
                ).start()

            return c

        lax.fori_loop(0, NY * NZ, send_slab, 0)

    def turn(n, c):
        @pl.when((n == 0) == low)
        def _():
            prepare()

        @pl.when((n == 0) != low)
        def _():
            send_all()

        return c

    lax.fori_loop(0, 2, turn, 0)

    def wait_all(ref, sem):
        pltpu.make_async_copy(ref, ref, sem).wait()

    def convert(first):
        for d in range(dirs):
            made = jnp.dot(rows[...], m2p_pad[d], preferred_element_type=F32)
            planes[d, first : first + TILE] = made.astype(BF16)

    def add_shifted(tiles, d):
        table = planes[d, : len(tiles) * TILE]
        real = acc[d, :, :LANES]
        imaginary = acc[d, :, LANES:]
        for j0 in range(0, slots, STACK):
            hot = jnp.concatenate([hot_rows(tiles, d, j) for j in range(j0, j0 + STACK)], axis=0)
            picked = jnp.dot(hot, table, preferred_element_type=F32)
            for n in range(STACK):
                j = j0 + n
                sr, si = shift_pad[d, j : j + 1, :LANES], shift_pad[d, j : j + 1, LANES:]
                pr, pi = picked[n * cap : (n + 1) * cap, :LANES], picked[n * cap : (n + 1) * cap, LANES:]
                real = real + sr * pr - si * pi
                imaginary = imaginary + sr * pi + si * pr
        acc[d, :, :LANES] = real
        acc[d, :, LANES:] = imaginary

    wait_all(sib_recv.at[pl.ds(0, NSIB - 1)], sib_sem)
    rows[cap : cap + 64] = sib_recv[...].reshape(64, WIDE)
    convert(0)

    def home_step(d, c):
        add_shifted((0,), d)
        return c

    lax.fori_loop(0, dirs, home_step, 0)

    wait_all(recv.at[0, pl.ds(0, 31)], tile_sem.at[0])
    rows[...] = recv[side].reshape(TILE, WIDE)
    convert(0)
    wait_all(recv.at[0], tile_sem.at[1])
    rows[...] = recv[1 - side].reshape(TILE, WIDE)
    convert(TILE)

    def slab_step(d, c):
        add_shifted((1, 2), d)
        return c

    lax.fori_loop(0, dirs, slab_step, 0)

    total = jnp.zeros((mreal, cap), F32)
    for d in range(dirs):
        total = total + lax.dot_general(
            p2l_pad[d], acc[d].astype(BF16), (((1,), (1,)), ((), ())), preferred_element_type=F32
        )
    live = lax.broadcasted_iota(I32, (mreal, cap), 1) < count_ref[...]
    out_ref[...] = jnp.where(live, total, F32(0)).astype(BF16)

    wait_all(send.at[pl.ds(0, NY * NZ - 1)], send_sem)
    wait_all(sib_recv.at[pl.ds(0, NSIB - 1)], sib_send_sem)


def per_device(mult, lists, ghost, sibx, counts, m2p, shifts, p2l):
    mreal, cap = mult.shape
    dirs = lists.shape[0]
    width = m2p.shape[0]
    hbm = pl.BlockSpec(memory_space=pltpu.HBM)
    return pl.pallas_call(
        kernel,
        out_shape=jax.ShapeDtypeStruct((mreal, cap), BF16),
        in_specs=[hbm] * 8,
        out_specs=pl.BlockSpec(memory_space=pltpu.VMEM),
        scratch_shapes=[
            pltpu.VMEM((mreal, cap), BF16),
            pltpu.VMEM(ghost.shape, I32),
            pltpu.VMEM(sibx.shape, I32),
            pltpu.VMEM((1, 1), I32),
            pltpu.VMEM(lists.shape, I32),
            pltpu.VMEM((mreal, width), BF16),
            pltpu.VMEM(shifts.shape, F32),
            pltpu.VMEM((mreal, width), BF16),
            pltpu.VMEM((WIDE, cap), BF16),
            pltpu.VMEM((dirs, WIDE, TILE), BF16),
            pltpu.VMEM((dirs, mreal, TILE), BF16),
            pltpu.VMEM((dirs, 40, TILE), F32),
            pltpu.VMEM((dirs, cap, 40), F32),
            pltpu.VMEM((3, dirs, lists.shape[1], cap, LANES), BF16),
            pltpu.VMEM((NY * NZ, 8, WIDE), BF16),
            pltpu.VMEM((8, WIDE), BF16),
            pltpu.VMEM((TILE, WIDE), BF16),
            pltpu.VMEM((NSIB, 8, WIDE), BF16),
            pltpu.VMEM((2, NY * HALF, 8, WIDE), BF16),
            pltpu.VMEM((dirs, 2 * TILE, TILE), BF16),
            pltpu.VMEM((dirs, cap, TILE), F32),
            pltpu.SemaphoreType.DMA,
            pltpu.SemaphoreType.DMA,
            pltpu.SemaphoreType.DMA,
            pltpu.SemaphoreType.DMA((2,)),
            pltpu.SemaphoreType.DMA((8,)),
        ],
        compiler_params=pltpu.CompilerParams(
            collective_id=0, has_side_effects=True, vmem_limit_bytes=48 * 2**20
        ),
        cost_estimate=pl.CostEstimate(flops=12 * 10**9, bytes_accessed=3 * 10**6, transcendentals=0),
    )(mult, ghost, sibx, counts.reshape(1, 1), lists, m2p.T, shifts, p2l)


def solution(mesh):
    both = ("group", "ingroup")
    return jax.shard_map(
        per_device,
        mesh=mesh,
        in_specs=(P(None, both), P(None, None, both), P(both, None), P(both, None), P(both), P(), P(), P()),
        out_specs=P(None, both),
        check_vma=False,
    )
```

```python
import functools

import jax
import jax.numpy as jnp
from jax import lax
from jax.experimental import pallas as pl
from jax.experimental.pallas import tpu as pltpu
from jax.sharding import PartitionSpec as P

MESH = pl.DeviceIdType.MESH
BF16, F32, I32 = jnp.bfloat16, jnp.float32, jnp.int32

LANES = 128
TILE = 256
NY, NZ = 4, 16
NSIB = 8
STACK = 2
WIDE = 384
HALF = 8


def columns_of(row, count):
    wide = jnp.broadcast_to(row.astype(F32), (LANES, count))
    return jnp.concatenate([wide[:, c : c + LANES].T for c in range(0, count, LANES)], axis=0)


def kernel(
    mult_hbm, ghost_hbm, sibx_hbm, count_hbm, lists_hbm, m2p_hbm, shifts_hbm, p2l_hbm, out_ref,
    mult_ref, ghost_ref, sibx_ref, count_ref, lists_ref, m2p_ref, shifts_ref, p2l_ref,
    mult_pad, m2p_pad, p2l_pad, shift_pad, place_cols, places, send, sib_send, rows, sib_recv, recv, planes, acc,
    send_sem, sib_send_sem, sib_sem, tile_sem, load_sem,
):
    g = lax.axis_index("group")
    i = lax.axis_index("ingroup")
    y, z = g // NZ, lax.rem(g, NZ)
    low = z < HALF
    side = z // HALF
    slot = y * HALF + lax.rem(z, HALF)
    dirs, slots = lists_ref.shape[0], lists_ref.shape[1]
    mreal, cap = mult_ref.shape
    nodes = shifts_ref.shape[2] // 2

    barrier = pltpu.get_barrier_semaphore()

    loads = [
        pltpu.make_async_copy(src, dst, load_sem.at[n])
        for n, (src, dst) in enumerate((
            (ghost_hbm, ghost_ref), (mult_hbm, mult_ref), (sibx_hbm, sibx_ref), (count_hbm, count_ref),
            (lists_hbm, lists_ref), (m2p_hbm, m2p_ref), (shifts_hbm, shifts_ref), (p2l_hbm, p2l_ref),
        ))
    ]
    for load in loads[:4]:
        load.start()

    def greet_slab(n, c):
        slab = ((y + n) & (NY - 1)) * NZ + ((z + n // NY) & (NZ - 1))
        pl.semaphore_signal(barrier, 1, device_id=(slab, i), device_id_type=MESH)
        return c

    def greet_sibling(n, c):
        pl.semaphore_signal(barrier, 1, device_id=(g, (i + n) & (NSIB - 1)), device_id_type=MESH)
        return c

    lax.fori_loop(1, NY * NZ, greet_slab, 0)
    lax.fori_loop(1, NSIB, greet_sibling, 0)
    for load in loads[4:]:
        load.start()

    mult_pad[...] = jnp.zeros_like(mult_pad)
    for load in loads[:4]:
        load.wait()
    mult_pad[:mreal, :] = mult_ref[...]

    def pick(cols):
        lanes = lax.broadcasted_iota(I32, cols.shape, 1).astype(F32)
        hot = jnp.where(cols == lanes, F32(1), F32(0)).astype(BF16)
        made = lax.dot_general(hot, mult_pad[...], (((1,), (1,)), ((), ())), preferred_element_type=F32)
        return made.astype(BF16)

    n_ghost = ghost_ref.shape[1]
    send[...] = pick(columns_of(ghost_ref[...], n_ghost)).reshape(send.shape)
    sib_row = jnp.concatenate([sibx_ref[...], jnp.full((1, LANES - sibx_ref.shape[1]), -1, I32)], axis=1)
    sib_send[...] = pick(columns_of(sib_row, LANES)[: sib_send.shape[0]])
    sib_recv[i] = sib_send[...]
    recv[side, slot] = send[g]

    lower = lax.broadcasted_iota(I32, (cap, LANES), 1).astype(F32)
    upper = (lower + LANES).astype(BF16)
    lower = lower.astype(BF16)

    def hot_rows(tiles, d, j):
        halves = [
            jnp.where(lanes == places[tile, d, j], BF16(1), BF16(0)) for tile in tiles for lanes in (lower, upper)
        ]
        return jnp.concatenate(halves, axis=1)

    def prepare():
        rows[...] = jnp.zeros_like(rows)
        rows[:cap] = pick(lax.broadcasted_iota(I32, (LANES, LANES), 0).astype(F32))
        m2p_pad[...] = jnp.zeros_like(m2p_pad)
        p2l_pad[...] = jnp.zeros_like(p2l_pad)
        shift_pad[...] = jnp.zeros_like(shift_pad)
        acc[...] = jnp.zeros_like(acc)
        for load in loads[4:]:
            load.wait()
        for d in range(dirs):
            for h in range(2):
                at = (2 * d + h) * nodes
                m2p_pad[d, :mreal, h * LANES : h * LANES + nodes] = m2p_ref[:, at : at + nodes]
                p2l_pad[d, :, h * LANES : h * LANES + nodes] = p2l_ref[:, at : at + nodes]
                shift_pad[d, :slots, h * LANES : h * LANES + nodes] = shifts_ref[d, :, h * nodes : (h + 1) * nodes]
            lists = lists_ref[d]
            far = lists - (cap + NSIB * 4)
            near = lists - cap
            far_at = lax.shift_right_arithmetic(far, 7) * 64 + (far & 63)
            far_side = lax.shift_right_arithmetic(far, 6) & 1
            own_at = jnp.where(lists < cap, lists, cap + lax.shift_right_arithmetic(near, 2) * 8 + (near & 3))
            far_at = far_at + jnp.where(far_side == side, TILE, 2 * TILE)
            place = jnp.where(far < 0, own_at, far_at)
            place = jnp.concatenate([place, jnp.full((40 - slots, cap), -1, I32)], axis=0)
            place_cols[d] = place.astype(F32).T

        def spread(d, c):
            for j in range(slots):
                place = jnp.broadcast_to(place_cols[d, :, j : j + 1], (cap, LANES))
                for tile in range(3):
                    places[tile, d, j] = (place - F32(tile * TILE)).astype(BF16)
            return c

        lax.fori_loop(0, dirs, spread, 0)

    def send_all():
        pl.semaphore_wait(barrier, NY * NZ - 1 + NSIB - 1)

        def send_sib(n, c):
            pltpu.make_async_remote_copy(
                src_ref=sib_send,
                dst_ref=sib_recv.at[i],
                send_sem=sib_send_sem,
                recv_sem=sib_sem,
                device_id=(g, (i + n) & (NSIB - 1)),
                device_id_type=MESH,
            ).start()
            return c


        def send_slab(n, c):
            to_z = (n // (NY * HALF)) * HALF + ((n // NY + z) & (HALF - 1))
            slab = ((y + n) & (NY - 1)) * NZ + to_z

            @pl.when(slab != g)
            def _():
                pltpu.make_async_remote_copy(
                    src_ref=send.at[slab],
                    dst_ref=recv.at[side, slot],
                    send_sem=send_sem,
                    recv_sem=tile_sem.at[jnp.where(to_z // HALF == side, 0, 1)],
                    device_id=(slab, i),
                    device_id_type=MESH,
                ).start()

            return c

        lax.fori_loop(0, NY * NZ, send_slab, 0)
        lax.fori_loop(1, NSIB, send_sib, 0)

    def turn(n, c):
        @pl.when((n == 0) == low)
        def _():
            prepare()

        @pl.when((n == 0) != low)
        def _():
            send_all()

        return c

    lax.fori_loop(0, 2, turn, 0)

    def wait_all(ref, sem):
        pltpu.make_async_copy(ref, ref, sem).wait()

    def convert(first):
        for d in range(dirs):
            made = jnp.dot(rows[...], m2p_pad[d], preferred_element_type=F32)
            planes[d, first : first + TILE] = made.astype(BF16)

    def add_shifted(tiles, d):
        table = planes[d, : len(tiles) * TILE]
        real = acc[d, :, :LANES]
        imaginary = acc[d, :, LANES:]
        for j0 in range(0, slots, STACK):
            hot = jnp.concatenate([hot_rows(tiles, d, j) for j in range(j0, j0 + STACK)], axis=0)
            picked = jnp.dot(hot, table, preferred_element_type=F32)
            for n in range(STACK):
                j = j0 + n
                sr, si = shift_pad[d, j : j + 1, :LANES], shift_pad[d, j : j + 1, LANES:]
                pr, pi = picked[n * cap : (n + 1) * cap, :LANES], picked[n * cap : (n + 1) * cap, LANES:]
                real = real + sr * pr - si * pi
                imaginary = imaginary + sr * pi + si * pr
        acc[d, :, :LANES] = real
        acc[d, :, LANES:] = imaginary

    wait_all(sib_recv.at[pl.ds(0, NSIB - 1)], sib_sem)
    rows[cap : cap + 64] = sib_recv[...].reshape(64, WIDE)
    convert(0)

    def home_step(d, c):
        add_shifted((0,), d)
        return c

    lax.fori_loop(0, dirs, home_step, 0)

    wait_all(recv.at[0, pl.ds(0, 31)], tile_sem.at[0])
    rows[...] = recv[side].reshape(TILE, WIDE)
    convert(0)
    wait_all(recv.at[0], tile_sem.at[1])
    rows[...] = recv[1 - side].reshape(TILE, WIDE)
    convert(TILE)

    def slab_step(d, c):
        add_shifted((1, 2), d)
        return c

    lax.fori_loop(0, dirs, slab_step, 0)

    total = jnp.zeros((mreal, cap), F32)
    for d in range(dirs):
        total = total + lax.dot_general(
            p2l_pad[d], acc[d].astype(BF16), (((1,), (1,)), ((), ())), preferred_element_type=F32
        )
    live = lax.broadcasted_iota(I32, (mreal, cap), 1) < count_ref[...]
    out_ref[...] = jnp.where(live, total, F32(0)).astype(BF16)

    wait_all(send.at[pl.ds(0, NY * NZ - 1)], send_sem)
    wait_all(sib_recv.at[pl.ds(0, NSIB - 1)], sib_send_sem)


def per_device(mult, lists, ghost, sibx, counts, m2p, shifts, p2l):
    mreal, cap = mult.shape
    dirs = lists.shape[0]
    width = m2p.shape[0]
    hbm = pl.BlockSpec(memory_space=pltpu.HBM)
    return pl.pallas_call(
        kernel,
        out_shape=jax.ShapeDtypeStruct((mreal, cap), BF16),
        in_specs=[hbm] * 8,
        out_specs=pl.BlockSpec(memory_space=pltpu.VMEM),
        scratch_shapes=[
            pltpu.VMEM((mreal, cap), BF16),
            pltpu.VMEM(ghost.shape, I32),
            pltpu.VMEM(sibx.shape, I32),
            pltpu.VMEM((1, 1), I32),
            pltpu.VMEM(lists.shape, I32),
            pltpu.VMEM((mreal, width), BF16),
            pltpu.VMEM(shifts.shape, F32),
            pltpu.VMEM((mreal, width), BF16),
            pltpu.VMEM((WIDE, cap), BF16),
            pltpu.VMEM((dirs, WIDE, TILE), BF16),
            pltpu.VMEM((dirs, mreal, TILE), BF16),
            pltpu.VMEM((dirs, 40, TILE), F32),
            pltpu.VMEM((dirs, cap, 40), F32),
            pltpu.VMEM((3, dirs, lists.shape[1], cap, LANES), BF16),
            pltpu.VMEM((NY * NZ, 8, WIDE), BF16),
            pltpu.VMEM((8, WIDE), BF16),
            pltpu.VMEM((TILE, WIDE), BF16),
            pltpu.VMEM((NSIB, 8, WIDE), BF16),
            pltpu.VMEM((2, NY * HALF, 8, WIDE), BF16),
            pltpu.VMEM((dirs, 2 * TILE, TILE), BF16),
            pltpu.VMEM((dirs, cap, TILE), F32),
            pltpu.SemaphoreType.DMA,
            pltpu.SemaphoreType.DMA,
            pltpu.SemaphoreType.DMA,
            pltpu.SemaphoreType.DMA((2,)),
            pltpu.SemaphoreType.DMA((8,)),
        ],
        compiler_params=pltpu.CompilerParams(
            collective_id=0, has_side_effects=True, vmem_limit_bytes=48 * 2**20
        ),
        cost_estimate=pl.CostEstimate(flops=12 * 10**9, bytes_accessed=3 * 10**6, transcendentals=0),
    )(mult, ghost, sibx, counts.reshape(1, 1), lists, m2p.T, shifts, p2l)


def solution(mesh):
    both = ("group", "ingroup")
    return jax.shard_map(
        per_device,
        mesh=mesh,
        in_specs=(P(None, both), P(None, None, both), P(both, None), P(both, None), P(both), P(), P(), P()),
        out_specs=P(None, both),
        check_vma=False,
    )
```
